128 devices in a mesh: samp: 16 (over y, z), feat: 8 (over x, core).
Axes of the slice: x: 4, y: 4, z: 4, core: 2. Of those that a mesh axis runs over, the one named last changes fastest.
Arguments:
- samples: bfloat16 [32768, 16384], P('samp', 'feat'), may hold values from -6 to 6
- residual_in: float32 [32768, 128], P('samp'), may hold values from -6 to 6
- weights_in: float32 [16384, 128], P('feat'), may hold values from -6 to 6
- inverses: float32 [8, 2048, 2048], P('feat', 'samp'), as said below
- order: int32 [6], replicated, may hold values from 0 to 7
Outputs:
- weights: float32 [16384, 128], P('feat')
- residual: float32 [32768, 128], P('samp')
The draws below stay inside these ranges and needn't reach their ends.
Inputs may be any that keep to these rules, and one draw needn't show every extreme that they name: The inverses are full symmetric positive definite matrices; diagonal entries lie between 0.5 / 32768 and 2 / 32768, and off-diagonal entries are about 0.4 / sqrt(2048) of the diagonal scale.
All inputs are finite; a program needn't handle non-finite values.
Results may differ from the reference program's by a relative error of at most 0.009.
Values sent between devices are 32-bit elements; how exact they have to be, the bound alone decides.
A program may use at most 64 MiB of HBM per device.

```python
import jax
import jax.numpy as jnp
from jax import lax

FB = 2048
OUTS = 128
STEPS = 6
NROWS = 32768
NBLOCK = 8
FEATS = 16384


def draw_inverses(key, part):
    key = jax.random.fold_in(key, 7)
    key_diag, key_off = jax.random.split(key)
    diag = jnp.exp(jax.random.uniform(key_diag, (NBLOCK, FB), jnp.float32, jnp.log(0.5), jnp.log(2.0)))
    off = jax.random.normal(key_off, (NBLOCK, FB, FB), jnp.float32)
    off = (off + jnp.transpose(off, (0, 2, 1))) * 0.5 ** 0.5
    scales = jnp.sqrt(diag[:, :, None] * diag[:, None, :])
    rows = jnp.arange(FB)[None, :, None]
    cols = jnp.arange(FB)[None, None, :]
    full = jnp.where(rows == cols, scales, off * scales * (0.4 / FB ** 0.5))
    return (full / NROWS).astype(jnp.float32)


def touch_ends(result, key, smallest, top_value):
    spot = [jax.random.randint(jax.random.fold_in(key, axis), (), 0, length) for axis, length in enumerate(result.shape)]
    main_axis = result.shape.index(max(result.shape))
    beside = spot[:main_axis] + [(spot[main_axis] + 1) % result.shape[main_axis]] + spot[main_axis + 1:]
    return result.at[tuple(spot)].set(smallest).at[tuple(beside)].set(top_value)


def level_of(stream_key, extent, cuts, low, top_value):
    def one(dim, shards_of):
        steps = jax.random.uniform(jax.random.fold_in(jax.random.fold_in(stream_key, 6), dim), (shards_of,), jnp.float32, low / len(cuts), top_value / len(cuts))
        return jnp.repeat(jnp.exp(steps), extent[dim] // shards_of).reshape((-1,) + (1,) * (len(extent) - dim - 1))

    loudness = one(*cuts[0])
    for cut in cuts[1:]:
        loudness = loudness * one(*cut)
    return loudness


def bell_draw(key, shape, deviation, reach, pieces=(), dtype=jnp.bfloat16):
    values = deviation * jax.random.normal(key, shape, jnp.float32)
    if pieces:
        values = values * level_of(key, shape, pieces, -0.22, 0.18)
    return jnp.clip(values, -reach, reach).astype(dtype)


def setup_inputs(seed: int = 0) -> dict:
    seeds = jax.random.split(jax.random.key(seed), 6)
    samples = bell_draw(seeds[0], (NROWS, FEATS), 1.0, 6.0, ((0, 16), (1, 8)))
    residual_in = bell_draw(seeds[1], (NROWS, OUTS), 1.0, 6.0, ((0, 16),), jnp.float32)
    weights_in = bell_draw(seeds[2], (FEATS, OUTS), 1.0, 6.0, ((0, 8),), jnp.float32)
    inverses = draw_inverses(jax.random.fold_in(seeds[5], 71), 0)
    order = touch_ends(jax.random.randint(seeds[4], (STEPS,), 0, NBLOCK), jax.random.fold_in(seeds[4], 1), 0, NBLOCK - 1).astype(jnp.int32)
    return dict(samples=samples, residual_in=residual_in, weights_in=weights_in, inverses=inverses, order=order)


def reference(samples, residual_in, weights_in, inverses, order):
    penalty = NROWS / 64.0
    weights = weights_in
    residual = residual_in
    for step in range(STEPS):
        block = order[step]
        start = (block * FB).astype(jnp.int32)
        columns = lax.dynamic_slice_in_dim(samples, start, FB, 1)
        current = lax.dynamic_slice_in_dim(weights, start, FB, 0)
        grad = lax.dot_general(columns, residual.astype(jnp.bfloat16), (((0,), (0,)), ((), ())), preferred_element_type=jnp.float32)
        grad = grad - penalty * current
        inverse = lax.dynamic_index_in_dim(inverses, block, 0, keepdims=False)
        delta = jnp.dot(inverse, grad, precision=lax.Precision.HIGHEST, preferred_element_type=jnp.float32)
        weights = lax.dynamic_update_slice_in_dim(weights, current + delta, start, 0)
        residual = residual - jnp.dot(columns, delta.astype(jnp.bfloat16), preferred_element_type=jnp.float32)
    return weights, residual
```

```python
import functools

import jax
import jax.numpy as jnp
from jax import lax
from jax.experimental import pallas as pl
from jax.experimental.pallas import tpu as pltpu
from jax.sharding import PartitionSpec as P

STEPS = 6
STREAMS = 4
FAR_FIRST = (2, 1, 3)
PIECES = 16
MESH = pl.DeviceIdType.MESH
F32 = jnp.float32
BF16 = jnp.bfloat16

M_RS = 0
M_AR = 2
M_DP = 4
M_AG = 6
M_X1 = 8
M_X2 = 10
N_SEM = 12
CHUNKS = 1


def nn(a, b):
    return jnp.dot(a, b, preferred_element_type=F32)


def nt(a, b):
    return lax.dot_general(a, b, (((1,), (1,)), ((), ())), preferred_element_type=F32)


def kernel(
    penalty, order_ref, x_hbm, r_hbm, w_hbm, inv_hbm, r, w, r_in, w_in, inv_in,
    x_buf, xb, xs, xr, rs, rb, rb0, gp, rsb, ao, arb, dpb, d_buf, cm, x1, x1s, x2,
    cs, cr, bf, bh, load_sem, ssem, rsem, isend, irecv, osend, orecv, csend, crecv,
):
    streams, stream, rows = rb.shape
    feats = w.shape[2]
    half, quarter = stream // 2, stream // 4
    blk, rblk = feats // 4, rows // CHUNKS
    k = lax.axis_index("samp")
    f = lax.axis_index("feat")
    y, z = k // 4, k % 4
    x, core = f // 2, f % 2
    other = x * 2 + 1 - core
    sib = (k, other)

    def zdev(t, feat=f):
        return (y * 4 + t, feat)

    def ydev(t, feat=f):
        return (t * 4 + z, feat)

    xdev = [(k, (x + 1 - 2 * (x % 2)) * 2 + core), (k, (3 - x) * 2 + core)]
    first = [(z, zdev), (y, ydev)]
    second = [(y, ydev), (z, zdev)]

    def at(pos, size):
        return pl.ds(pl.multiple_of(pos * size, size), size)

    def outs_of(core_of, q):
        return pl.ds(pl.multiple_of(core_of * half + q * quarter, quarter), quarter)

    def hrows(q):
        return pl.ds(q * half, half)

    def load(src, dst, i):
        c = pltpu.make_async_copy(src, dst, load_sem.at[i])
        c.start()
        return c

    inv_load = load(inv_hbm, inv_in, 5)
    r_load = load(r_hbm, r_in, 6)
    loads = []
    for b in range(4):
        cols = pl.ds(b * blk, blk)
        loads.append(load(x_hbm.at[:, cols], x_buf.at[:, cols], b))
    w_load = load(w_hbm, w_in, 7)

    barrier = pltpu.get_barrier_semaphore()
    partners = [sib, xdev[0], xdev[1]]
    for d in (1, 2, 3):
        for feat in (f, other):
            partners += [zdev((z + d) % 4, feat), ydev((y + d) % 4, feat)]
    for dev in partners:
        pl.semaphore_signal(barrier, inc=1, device_id=dev, device_id_type=MESH)

    r_load.wait()
    turned = r_in[...].T
    r[...] = turned.reshape(r.shape)
    rb0[...] = turned.astype(BF16)
    pl.semaphore_wait(barrier, len(partners))

    def inv_copy(d, src, dst, dev):
        return pltpu.make_async_remote_copy(src, dst, isend.at[d], irecv.at[d], dev, MESH)

    def inv_piece(core_of, d):
        return bf.at[core_of, at((z + 4 - d) % 4, blk // 4)]

    inv_load.wait()
    for d in (1, 2, 3):
        t = (z + d) % 4
        inv_copy(d, inv_in.at[:, at(t, blk)], inv_piece(core, 0), zdev(t)).start()
    bf[core, at(z, blk // 4)] = inv_in[:, at(z, blk)]
    inv_copy(4, inv_piece(core, 0), inv_piece(core, 0), sib).start()


    mine = at(core, rows)
    its = at(1 - core, rows)

    piece = rows // PIECES

    def half_copy(b):
        part = at(b, piece)
        return pltpu.make_async_remote_copy(xs.at[part], xr.at[part], osend.at[b], orecv.at[b], sib, MESH)

    def send_half(b):
        here = pl.ds(pl.multiple_of((1 - core) * rows + b * piece, piece), piece)
        xs[at(b, piece)] = x_buf[here].astype(F32)
        half_copy(b).start()

    def take_half(b):
        half_copy(b).wait()
        xb[1 - core, at(b, piece)] = xr[at(b, piece)].astype(BF16)

    class Step:
        def __init__(self, t):
            self.u, self.s = lax.rem(t, streams), t // streams
            self.slot = lax.rem(self.s, 2)
            self.order = order_ref[self.s]
            self.parity = lax.rem(self.order, 2)
            self.own = jnp.where(self.order == f, 1.0, 0.0).astype(F32)
            self.near = jnp.where(self.order - self.parity == 2 * x, 1.0, 0.0).astype(F32)

        def copy(self, num, src, dst, dev):
            here = self.u, self.slot
            return pltpu.make_async_remote_copy(src, dst, ssem.at[here], rsem.at[(*here, num)], dev, MESH)

        def send(self, num, src, dst, dev):
            self.copy(num, src, dst, dev).start()

        def arrived(self, num, dst):
            self.copy(num, dst, dst, sib).wait_recv()

        def all_left(self):
            sent = xr.at[pl.ds(0, (40 * quarter * blk + 2 * stream * rows) // feats)]
            self.copy(0, sent, sent, sib).wait_send()

        def gradient(self):
            u, slot = self.u, self.slot
            for pair in (1 - z // 2, z // 2):
                cols = at(pair, 2 * blk)
                g = nn(rb[u], xb[self.parity, :, cols])
                gp[u, :, cols] = self.near * g - self.own * penalty * w[u, :, cols]
                for b in (pair * 2, pair * 2 + 1):
                    cols = at(b, blk)
                    d = (b + 4 - z) % 4
                    self.send(M_RS, gp.at[u, outs_of(1 - core, 0), cols], rsb.at[u, slot, 0, 3 + d], zdev(b, other))
                    d = (b + 4 - y) % 4
                    self.send(M_RS + 1, gp.at[u, outs_of(1 - core, 1), cols], rsb.at[u, slot, 1, 3 + d], ydev(b, other))
            for d in FAR_FIRST:
                b = (z + d) % 4
                self.send(M_RS, gp.at[u, outs_of(core, 0), at(b, blk)], rsb.at[u, slot, 0, d - 1], zdev(b))
                b = (y + d) % 4
                self.send(M_RS + 1, gp.at[u, outs_of(core, 1), at(b, blk)], rsb.at[u, slot, 1, d - 1], ydev(b))

        def scatter(self, b, value):
            u, slot = self.u, self.slot
            cols = pl.ds(b * blk, blk)
            gp[u, :, cols] = value
            for q in range(2):
                pos, dev = first[q]
                d = (b + 4 - pos) % 4
                self.send(
                    M_RS + q, gp.at[u, outs_of(1 - core, q), cols], rsb.at[u, slot, q, 3 + d], dev(b, other)
                )

                @pl.when(d != 0)
                def _():
                    self.send(M_RS + q, gp.at[u, outs_of(core, q), cols], rsb.at[u, slot, q, d - 1], dev(b))

        def reduce(self):
            u, slot = self.u, self.slot
            for q in range(2):
                self.arrived(M_RS + q, rsb.at[u, slot, q])
                acc = gp[u, outs_of(core, q), at(first[q][0], blk)]
                for i in range(7):
                    acc = acc + rsb[u, slot, q, i]
                ao[u, q] = acc
                pos, dev = second[q]
                for d in FAR_FIRST:
                    self.send(M_AR + q, ao.at[u, q], arb.at[u, slot, q, d - 1], dev((pos + d) % 4))

        def multiply(self):
            u, slot = self.u, self.slot
            for q in range(2):
                self.arrived(M_AR + q, arb.at[u, slot, q])
                acc = ao[u, q] + arb[u, slot, q, 0] + arb[u, slot, q, 1] + arb[u, slot, q, 2]
                hi = acc.astype(BF16).astype(F32)
                both = jnp.concatenate([hi, acc - hi], axis=0).astype(BF16)
                dot = nt if q == 0 else nn
                whole = dot(both, bh[self.parity])
                pos, dev = first[q]
                dpb[u, slot, q, pos] = whole[:quarter] + whole[quarter:]
                here = dpb.at[u, slot, q, pos]
                for d in FAR_FIRST:
                    self.send(M_DP + q, here, here, dev((pos + d) % 4))

        def gather(self):
            u, slot = self.u, self.slot
            for q in range(2):
                self.arrived(M_DP + q, arb.at[u, slot, q])
                pos, dev = second[q]
                here = d_buf.at[u, slot, outs_of(core, q), at(pos, blk)]
                here[...] = (dpb[u, slot, q, 0] + dpb[u, slot, q, 1]) + (dpb[u, slot, q, 2] + dpb[u, slot, q, 3])
                for d in FAR_FIRST:
                    for feat in (f, other):
                        self.send(M_AG + q, here, here, dev((pos + d) % 4, feat))
                self.send(M_AG + q, here, here, sib)

        def gathered(self):
            u, slot = self.u, self.slot
            for q in range(2):
                self.arrived(M_AG + q, rsb.at[u, slot, q])
            w[u] += self.own * d_buf[u, slot]

        def change(self):
            db = d_buf[self.u, self.slot].astype(BF16)
            for b in range(CHUNKS):
                self.exchange(b, self.near * nt(db, xb[self.parity, pl.ds(b * rblk, rblk), :]))

        def merge(self, b):
            here = (self.u, slice(None), pl.ds(b * rblk, rblk))
            sems = csend.at[self.u, b], crecv.at[self.u, b]
            return pltpu.make_async_remote_copy(cs.at[here], cr.at[here], *sems, sib, MESH)

        def first_change(self):
            u, slot = self.u, self.slot
            db = d_buf[u, slot].astype(BF16)

            def part(core_of, b):
                here = pl.ds(pl.multiple_of(core_of * rows + b * rblk, rblk), rblk)
                return self.own * nt(db, x_buf[here, :])

            for b in range(CHUNKS):
                cs[u, :, pl.ds(b * rblk, rblk)] = part(1 - core, b)
                self.merge(b).start()
            for b in range(CHUNKS):
                cm[u, :, pl.ds(b * rblk, rblk)] = part(core, b)

        def first_merge(self):
            for b in range(CHUNKS):
                cols = pl.ds(b * rblk, rblk)
                self.merge(b).wait()
                self.exchange(b, cm[self.u, :, cols] + cr[self.u, :, cols])

        def exchange(self, b, value):
            u, slot = self.u, self.slot
            cols = pl.ds(b * rblk, rblk)
            cm[u, :, cols] = value
            for q in range(2):
                self.send(M_X1 + b, cm.at[u, hrows(q), cols], x1.at[u, slot, hrows(q), cols], xdev[q])

        def exchange2(self):
            u, slot = self.u, self.slot
            for b in range(CHUNKS):
                cols = pl.ds(b * rblk, rblk)
                self.arrived(M_X1 + b, x1.at[u, slot, :, cols])
                x1s[u, :, cols] = cm[u, :, cols] + x1[u, slot, :, cols]
                for q in range(2):
                    self.send(M_X2 + b, x1s.at[u, hrows(q), cols], x2.at[u, slot, hrows(q), cols], xdev[1 - q])

        def total(self):
            u, slot = self.u, self.slot
            for b in range(CHUNKS):
                cols = pl.ds(b * rblk, rblk)
                here = (u, slice(None), pl.ds(pl.multiple_of(core * rows + b * rblk, rblk), rblk))
                self.arrived(M_X2 + b, x2.at[u, slot, :, cols])
                new = r[here] - (x1s[u, :, cols] + x2[u, slot, :, cols])
                r[here] = new
                rb[u, :, cols] = new.astype(BF16)

    def give_rows(u):
        sems = osend.at[PIECES + u], orecv.at[PIECES + u]
        return pltpu.make_async_remote_copy(r.at[u, :, mine], r.at[u, :, mine], *sems, sib, MESH)

    steps = [Step(jnp.int32(u)) for u in range(streams)]
    for b in range(4):
        cols = pl.ds(b * blk, blk)
        loads[b].wait()
        if b == 0:
            w_load.wait()
        w[:, :, cols] = w_in[cols, :].T.reshape(streams, stream, blk)
        g = nn(rb0[...], x_buf[:, cols])
        for u in range(streams):
            part = g[u * stream:(u + 1) * stream]
            steps[u].scatter(b, steps[u].own * (part - penalty * w[u, :, cols]))
    for b in range(5):
        send_half(b)
    for d in (1, 3, 2):
        here = inv_piece(core, d)
        inv_copy(d, here, here, sib).wait()
        inv_copy(4 + d, here, here, sib).start()
    for b in range(5, 10):
        send_half(b)
    own_half = load(x_hbm.at[at(core, rows)], xb.at[core], 4)

    starts = STEPS * streams

    def quarter_step(t, carry, edge):
        def when(lo, hi, part):
            if edge:
                pl.when((t >= lo) & (t < hi))(part)
            else:
                part()

        a, b, c, d = (Step(jnp.clip(t - i, 0, starts - 1)) for i in range(4))
        if edge:
            when(streams, starts, a.gradient)
        else:
            a.gradient()
        when(3, starts + 3, d.exchange2)
        when(1, starts + 1, b.multiply)
        when(2, starts + 2, c.gathered)
        if edge:
            when(2, streams + 2, c.first_change)
        when(streams + 2, starts + 2, c.change)
        when(0, starts, a.reduce)
        if edge:
            when(2, streams + 2, c.first_merge)
        when(1, starts + 1, b.gather)
        when(3, starts + 3, d.total)
        when(3, starts + 3, d.all_left)
        return carry

    def take_inverse():
        for d in range(4):
            inv_copy(4 + d, inv_piece(core, d), inv_piece(core, d), sib).wait_send()
            inv_copy(4 + d, inv_piece(1 - core, d), inv_piece(1 - core, d), sib).wait_recv()
        for o in range(2):
            bh[o] = bf[o].astype(BF16)

    def take_samples(lo, hi):
        def take(b, carry):
            take_half(b)
            return carry

        lax.fori_loop(lo, hi, take, 0)

    def first_quarter_step(t, carry):
        pl.when(t == 1)(take_inverse)
        pl.when(t == streams)(own_half.wait)
        pl.when(t == streams)(functools.partial(take_samples, 9, PIECES))
        quarter_step(t, carry, True)
        pl.when(t == 2)(functools.partial(take_samples, 0, 5))
        pl.when(t == 3)(functools.partial(take_samples, 5, 9))

        @pl.when(t < 3)
        def _():
            for i in range(2):
                send_half(10 + t * 2 + i)

        return carry

    def last_quarter_step(t, carry):
        quarter_step(t, carry, True)
        give_rows(lax.rem(t - 3, streams)).start()
        return carry

    lax.fori_loop(0, streams + 2, first_quarter_step, 0)
    lax.fori_loop(streams + 2, starts - 1, functools.partial(quarter_step, edge=False), 0)
    lax.fori_loop(starts - 1, starts + 3, last_quarter_step, 0)
    for u in range(streams):
        there = r.at[u, :, its]
        sems = osend.at[PIECES + u], orecv.at[PIECES + u]
        give_rows(u).wait_send()
        pltpu.make_async_remote_copy(there, there, *sems, sib, MESH).wait_recv()


def on_device(samples, residual_in, weights_in, inverses, order):
    chip_rows, feats = samples.shape
    outs = residual_in.shape[1]
    rows = chip_rows // 2
    stream = outs // STREAMS
    quarter = stream // 4
    blk = feats // 4
    samp = lax.axis_size("samp")
    penalty = chip_rows * samp / 64.0 / samp
    vmem = pl.BlockSpec(memory_space=pltpu.VMEM)
    smem = pl.BlockSpec(memory_space=pltpu.SMEM)
    per_rows = (STREAMS, stream, rows)
    per_chip = (STREAMS, stream, chip_rows)
    per_feats = (STREAMS, stream, feats)
    residual, weights = pl.pallas_call(
        functools.partial(kernel, penalty),
        out_shape=[jax.ShapeDtypeStruct(per_chip, F32), jax.ShapeDtypeStruct(per_feats, F32)],
        in_specs=[smem] + [pl.BlockSpec(memory_space=pl.ANY)] * 4,
        out_specs=[vmem, vmem],
        scratch_shapes=[
            pltpu.VMEM((chip_rows, outs), F32),
            pltpu.VMEM((feats, outs), F32),
            pltpu.VMEM((blk // 4, feats), F32),
            pltpu.VMEM((chip_rows, feats), BF16),
            pltpu.VMEM((2, rows, feats), BF16),
            pltpu.VMEM((rows, feats), F32),
            pltpu.VMEM((rows, feats), F32),
            pltpu.VMEM(per_rows, F32),
            pltpu.VMEM(per_rows, BF16),
            pltpu.VMEM((outs, chip_rows), BF16),
            pltpu.VMEM(per_feats, F32),
            pltpu.VMEM((STREAMS, 2, 2, 7, quarter, blk), F32),
            pltpu.VMEM((STREAMS, 2, quarter, blk), F32),
            pltpu.VMEM((STREAMS, 2, 2, 3, quarter, blk), F32),
            pltpu.VMEM((STREAMS, 2, 2, 4, quarter, blk), F32),
            pltpu.VMEM((STREAMS, 2, stream, feats), F32),
            pltpu.VMEM(per_rows, F32),
            pltpu.VMEM((STREAMS, 2, stream, rows), F32),
            pltpu.VMEM(per_rows, F32),
            pltpu.VMEM((STREAMS, 2, stream, rows), F32),
            pltpu.VMEM(per_rows, F32),
            pltpu.VMEM(per_rows, F32),
            pltpu.VMEM((2, blk, blk), F32),
            pltpu.VMEM((2, blk, blk), BF16),
            pltpu.SemaphoreType.DMA((8,)),
            pltpu.SemaphoreType.DMA((STREAMS, 2)),
            pltpu.SemaphoreType.DMA((STREAMS, 2, N_SEM)),
            pltpu.SemaphoreType.DMA((8,)),
            pltpu.SemaphoreType.DMA((8,)),
            pltpu.SemaphoreType.DMA((PIECES + STREAMS,)),
            pltpu.SemaphoreType.DMA((PIECES + STREAMS,)),
            pltpu.SemaphoreType.DMA((STREAMS, CHUNKS)),
            pltpu.SemaphoreType.DMA((STREAMS, CHUNKS)),
        ],
        compiler_params=pltpu.CompilerParams(
            collective_id=0, has_side_effects=True, vmem_limit_bytes=56 * 1024 * 1024
        ),
        cost_estimate=pl.CostEstimate(
            flops=STEPS * 4 * rows * feats * outs, bytes_accessed=2 * chip_rows * feats, transcendentals=0
        ),
    )(order, samples, residual_in, weights_in, inverses[0])
    return weights.reshape(outs, feats).T, residual.reshape(outs, chip_rows).T


def solution(mesh):
    placed = (P("samp", "feat"), P("samp", None), P("feat", None), P("feat", "samp", None), P())
    return jax.shard_map(
        on_device,
        mesh=mesh,
        in_specs=placed,
        out_specs=(P("feat", None), P("samp", None)),
        check_vma=False,
    )
```

```python
import functools

import jax
import jax.numpy as jnp
from jax import lax
from jax.experimental import pallas as pl
from jax.experimental.pallas import tpu as pltpu
from jax.sharding import PartitionSpec as P

STEPS = 6
STREAMS = 4
FAR_FIRST = (2, 1, 3)
PIECES = 16
MESH = pl.DeviceIdType.MESH
F32 = jnp.float32
BF16 = jnp.bfloat16

M_RS = 0
M_AR = 2
M_DP = 4
M_AG = 6
M_X1 = 8
M_X2 = 10
N_SEM = 12
CHUNKS = 1


def nn(a, b):
    return jnp.dot(a, b, preferred_element_type=F32)


def nt(a, b):
    return lax.dot_general(a, b, (((1,), (1,)), ((), ())), preferred_element_type=F32)


def kernel(
    penalty, order_ref, x_hbm, r_hbm, w_hbm, inv_hbm, r, w, r_in, w_in, inv_in,
    x_buf, xb, xs, xr, rs, rb, rb0, gp, rsb, ao, arb, dpb, d_buf, cm, x1, x1s, x2,
    cs, cr, bf, bh, load_sem, ssem, rsem, isend, irecv, osend, orecv, csend, crecv,
):
    streams, stream, rows = rb.shape
    feats = w.shape[2]
    half, quarter = stream // 2, stream // 4
    blk, rblk = feats // 4, rows // CHUNKS
    k = lax.axis_index("samp")
    f = lax.axis_index("feat")
    y, z = k // 4, k % 4
    x, core = f // 2, f % 2
    other = x * 2 + 1 - core
    sib = (k, other)

    def zdev(t, feat=f):
        return (y * 4 + t, feat)

    def ydev(t, feat=f):
        return (t * 4 + z, feat)

    xdev = [(k, (x + 1 - 2 * (x % 2)) * 2 + core), (k, (3 - x) * 2 + core)]
    first = [(z, zdev), (y, ydev)]
    second = [(y, ydev), (z, zdev)]

    def at(pos, size):
        return pl.ds(pl.multiple_of(pos * size, size), size)

    def outs_of(core_of, q):
        return pl.ds(pl.multiple_of(core_of * half + q * quarter, quarter), quarter)

    def hrows(q):
        return pl.ds(q * half, half)

    def load(src, dst, i):
        c = pltpu.make_async_copy(src, dst, load_sem.at[i])
        c.start()
        return c

    inv_load = load(inv_hbm, inv_in, 5)
    r_load = load(r_hbm, r_in, 6)
    loads = []
    for b in range(4):
        cols = pl.ds(b * blk, blk)
        loads.append(load(x_hbm.at[:, cols], x_buf.at[:, cols], b))
    w_load = load(w_hbm, w_in, 7)

    barrier = pltpu.get_barrier_semaphore()
    partners = [sib, xdev[0], xdev[1]]
    for d in (1, 2, 3):
        for feat in (f, other):
            partners += [zdev((z + d) % 4, feat), ydev((y + d) % 4, feat)]
    for dev in partners:
        pl.semaphore_signal(barrier, inc=1, device_id=dev, device_id_type=MESH)

    r_load.wait()
    turned = r_in[...].T
    r[...] = turned.reshape(r.shape)
    rb0[...] = turned.astype(BF16)
    pl.semaphore_wait(barrier, len(partners))

    def inv_copy(d, src, dst, dev):
        return pltpu.make_async_remote_copy(src, dst, isend.at[d], irecv.at[d], dev, MESH)

    def inv_piece(core_of, d):
        return bf.at[core_of, at((z + 4 - d) % 4, blk // 4)]

    inv_load.wait()
    for d in (1, 2, 3):
        t = (z + d) % 4
        inv_copy(d, inv_in.at[:, at(t, blk)], inv_piece(core, 0), zdev(t)).start()
    bf[core, at(z, blk // 4)] = inv_in[:, at(z, blk)]
    inv_copy(4, inv_piece(core, 0), inv_piece(core, 0), sib).start()


    mine = at(core, rows)
    its = at(1 - core, rows)

    piece = rows // PIECES

    def half_copy(b):
        part = at(b, piece)
        return pltpu.make_async_remote_copy(xs.at[part], xr.at[part], osend.at[b], orecv.at[b], sib, MESH)

    def send_half(b):
        here = pl.ds(pl.multiple_of((1 - core) * rows + b * piece, piece), piece)
        xs[at(b, piece)] = x_buf[here].astype(F32)
        half_copy(b).start()

    def take_half(b):
        half_copy(b).wait()
        xb[1 - core, at(b, piece)] = xr[at(b, piece)].astype(BF16)

    class Step:
        def __init__(self, t):
            self.u, self.s = lax.rem(t, streams), t // streams
            self.slot = lax.rem(self.s, 2)
            self.order = order_ref[self.s]
            self.parity = lax.rem(self.order, 2)
            self.own = jnp.where(self.order == f, 1.0, 0.0).astype(F32)
            self.near = jnp.where(self.order - self.parity == 2 * x, 1.0, 0.0).astype(F32)

        def copy(self, num, src, dst, dev):
            here = self.u, self.slot
            return pltpu.make_async_remote_copy(src, dst, ssem.at[here], rsem.at[(*here, num)], dev, MESH)

        def send(self, num, src, dst, dev):
            self.copy(num, src, dst, dev).start()

        def arrived(self, num, dst):
            self.copy(num, dst, dst, sib).wait_recv()

        def all_left(self):
            sent = xr.at[pl.ds(0, (40 * quarter * blk + 2 * stream * rows) // feats)]
            self.copy(0, sent, sent, sib).wait_send()

        def gradient(self):
            u, slot = self.u, self.slot
            for pair in (1 - z // 2, z // 2):
                cols = at(pair, 2 * blk)
                g = nn(rb[u], xb[self.parity, :, cols])
                gp[u, :, cols] = self.near * g - self.own * penalty * w[u, :, cols]
                for b in (pair * 2, pair * 2 + 1):
                    cols = at(b, blk)
                    d = (b + 4 - z) % 4
                    self.send(M_RS, gp.at[u, outs_of(1 - core, 0), cols], rsb.at[u, slot, 0, 3 + d], zdev(b, other))
                    d = (b + 4 - y) % 4
                    self.send(M_RS + 1, gp.at[u, outs_of(1 - core, 1), cols], rsb.at[u, slot, 1, 3 + d], ydev(b, other))
            for d in FAR_FIRST:
                b = (z + d) % 4
                self.send(M_RS, gp.at[u, outs_of(core, 0), at(b, blk)], rsb.at[u, slot, 0, d - 1], zdev(b))
                b = (y + d) % 4
                self.send(M_RS + 1, gp.at[u, outs_of(core, 1), at(b, blk)], rsb.at[u, slot, 1, d - 1], ydev(b))

        def scatter(self, b, value):
            u, slot = self.u, self.slot
            cols = pl.ds(b * blk, blk)
            gp[u, :, cols] = value
            for q in range(2):
                pos, dev = first[q]
                d = (b + 4 - pos) % 4
                self.send(
                    M_RS + q, gp.at[u, outs_of(1 - core, q), cols], rsb.at[u, slot, q, 3 + d], dev(b, other)
                )

                @pl.when(d != 0)
                def _():
                    self.send(M_RS + q, gp.at[u, outs_of(core, q), cols], rsb.at[u, slot, q, d - 1], dev(b))

        def reduce(self):
            u, slot = self.u, self.slot
            for q in range(2):
                self.arrived(M_RS + q, rsb.at[u, slot, q])
                acc = gp[u, outs_of(core, q), at(first[q][0], blk)]
                for i in range(7):
                    acc = acc + rsb[u, slot, q, i]
                ao[u, q] = acc
                pos, dev = second[q]
                for d in FAR_FIRST:
                    self.send(M_AR + q, ao.at[u, q], arb.at[u, slot, q, d - 1], dev((pos + d) % 4))

        def multiply(self):
            u, slot = self.u, self.slot
            for q in range(2):
                self.arrived(M_AR + q, arb.at[u, slot, q])
                acc = ao[u, q] + arb[u, slot, q, 0] + arb[u, slot, q, 1] + arb[u, slot, q, 2]
                hi = acc.astype(BF16).astype(F32)
                both = jnp.concatenate([hi, acc - hi], axis=0).astype(BF16)
                dot = nt if q == 0 else nn
                whole = dot(both, bh[self.parity])
                pos, dev = first[q]
                dpb[u, slot, q, pos] = whole[:quarter] + whole[quarter:]
                here = dpb.at[u, slot, q, pos]
                for d in FAR_FIRST:
                    self.send(M_DP + q, here, here, dev((pos + d) % 4))

        def gather(self):
            u, slot = self.u, self.slot
            for q in range(2):
                self.arrived(M_DP + q, arb.at[u, slot, q])
                pos, dev = second[q]
                here = d_buf.at[u, slot, outs_of(core, q), at(pos, blk)]
                here[...] = (dpb[u, slot, q, 0] + dpb[u, slot, q, 1]) + (dpb[u, slot, q, 2] + dpb[u, slot, q, 3])
                for d in FAR_FIRST:
                    for feat in (f, other):
                        self.send(M_AG + q, here, here, dev((pos + d) % 4, feat))
                self.send(M_AG + q, here, here, sib)

        def gathered(self):
            u, slot = self.u, self.slot
            for q in range(2):
                self.arrived(M_AG + q, rsb.at[u, slot, q])

        def weights(self):
            w[self.u] += self.own * d_buf[self.u, self.slot]

        def change(self):
            db = d_buf[self.u, self.slot].astype(BF16)
            for b in range(CHUNKS):
                self.exchange(b, self.near * nt(db, xb[self.parity, pl.ds(b * rblk, rblk), :]))

        def merge(self, b):
            here = (self.u, slice(None), pl.ds(b * rblk, rblk))
            sems = csend.at[self.u, b], crecv.at[self.u, b]
            return pltpu.make_async_remote_copy(cs.at[here], cr.at[here], *sems, sib, MESH)

        def first_change(self):
            u, slot = self.u, self.slot
            db = d_buf[u, slot].astype(BF16)

            def part(core_of, b):
                here = pl.ds(pl.multiple_of(core_of * rows + b * rblk, rblk), rblk)
                return self.own * nt(db, x_buf[here, :])

            for b in range(CHUNKS):
                cs[u, :, pl.ds(b * rblk, rblk)] = part(1 - core, b)
                self.merge(b).start()
            for b in range(CHUNKS):
                cm[u, :, pl.ds(b * rblk, rblk)] = part(core, b)

        def first_merge(self):
            for b in range(CHUNKS):
                cols = pl.ds(b * rblk, rblk)
                self.merge(b).wait()
                self.exchange(b, cm[self.u, :, cols] + cr[self.u, :, cols])

        def exchange(self, b, value):
            u, slot = self.u, self.slot
            cols = pl.ds(b * rblk, rblk)
            cm[u, :, cols] = value
            for q in range(2):
                self.send(M_X1 + b, cm.at[u, hrows(q), cols], x1.at[u, slot, hrows(q), cols], xdev[q])

        def exchange2(self):
            u, slot = self.u, self.slot
            for b in range(CHUNKS):
                cols = pl.ds(b * rblk, rblk)
                self.arrived(M_X1 + b, x1.at[u, slot, :, cols])
                x1s[u, :, cols] = cm[u, :, cols] + x1[u, slot, :, cols]
                for q in range(2):
                    self.send(M_X2 + b, x1s.at[u, hrows(q), cols], x2.at[u, slot, hrows(q), cols], xdev[1 - q])

        def total(self):
            u, slot = self.u, self.slot
            for b in range(CHUNKS):
                cols = pl.ds(b * rblk, rblk)
                here = (u, slice(None), pl.ds(pl.multiple_of(core * rows + b * rblk, rblk), rblk))
                self.arrived(M_X2 + b, x2.at[u, slot, :, cols])
                new = r[here] - (x1s[u, :, cols] + x2[u, slot, :, cols])
                r[here] = new
                rb[u, :, cols] = new.astype(BF16)

    def give_rows(u):
        sems = osend.at[PIECES + u], orecv.at[PIECES + u]
        return pltpu.make_async_remote_copy(r.at[u, :, mine], r.at[u, :, mine], *sems, sib, MESH)

    steps = [Step(jnp.int32(u)) for u in range(streams)]
    for b in range(4):
        cols = pl.ds(b * blk, blk)
        loads[b].wait()
        if b == 0:
            w_load.wait()
        w[:, :, cols] = w_in[cols, :].T.reshape(streams, stream, blk)
        g = nn(rb0[...], x_buf[:, cols])
        for u in range(streams):
            part = g[u * stream:(u + 1) * stream]
            steps[u].scatter(b, steps[u].own * (part - penalty * w[u, :, cols]))
    for b in range(5):
        send_half(b)
    for d in (1, 3, 2):
        here = inv_piece(core, d)
        inv_copy(d, here, here, sib).wait()
        inv_copy(4 + d, here, here, sib).start()
    for b in range(5, 10):
        send_half(b)
    own_half = load(x_hbm.at[at(core, rows)], xb.at[core], 4)

    starts = STEPS * streams

    def quarter_step(t, carry, edge):
        def when(lo, hi, part):
            if edge:
                pl.when((t >= lo) & (t < hi))(part)
            else:
                part()

        a, b, c, d = (Step(jnp.clip(t - i, 0, starts - 1)) for i in range(4))
        if edge:
            when(streams, starts, a.gradient)
        else:
            a.gradient()
        when(3, starts + 3, d.exchange2)
        when(1, starts + 1, b.multiply)
        when(2, starts + 2, c.gathered)
        if edge:
            when(2, streams + 2, c.first_change)
        when(streams + 2, starts + 2, c.change)
        when(0, starts, a.reduce)
        if edge:
            when(2, streams + 2, c.first_merge)
        when(1, starts + 1, b.gather)
        when(2, starts + 2, c.weights)
        when(3, starts + 3, d.total)
        when(3, starts + 3, d.all_left)
        return carry

    def take_inverse():
        for d in range(4):
            inv_copy(4 + d, inv_piece(core, d), inv_piece(core, d), sib).wait_send()
            inv_copy(4 + d, inv_piece(1 - core, d), inv_piece(1 - core, d), sib).wait_recv()
        for o in range(2):
            bh[o] = bf[o].astype(BF16)

    def take_samples(lo, hi):
        def take(b, carry):
            take_half(b)
            return carry

        lax.fori_loop(lo, hi, take, 0)

    def first_quarter_step(t, carry):
        pl.when(t == 1)(take_inverse)
        pl.when(t == streams)(own_half.wait)
        pl.when(t == streams)(functools.partial(take_samples, 9, PIECES))
        quarter_step(t, carry, True)
        pl.when(t == 2)(functools.partial(take_samples, 0, 5))
        pl.when(t == 3)(functools.partial(take_samples, 5, 9))

        @pl.when(t < 3)
        def _():
            for i in range(2):
                send_half(10 + t * 2 + i)

        return carry

    def last_quarter_step(t, carry):
        quarter_step(t, carry, True)
        give_rows(lax.rem(t - 3, streams)).start()
        return carry

    lax.fori_loop(0, streams + 2, first_quarter_step, 0)
    lax.fori_loop(streams + 2, starts - 1, functools.partial(quarter_step, edge=False), 0)
    lax.fori_loop(starts - 1, starts + 3, last_quarter_step, 0)
    for u in range(streams):
        there = r.at[u, :, its]
        sems = osend.at[PIECES + u], orecv.at[PIECES + u]
        give_rows(u).wait_send()
        pltpu.make_async_remote_copy(there, there, *sems, sib, MESH).wait_recv()


def on_device(samples, residual_in, weights_in, inverses, order):
    chip_rows, feats = samples.shape
    outs = residual_in.shape[1]
    rows = chip_rows // 2
    stream = outs // STREAMS
    quarter = stream // 4
    blk = feats // 4
    samp = lax.axis_size("samp")
    penalty = chip_rows * samp / 64.0 / samp
    vmem = pl.BlockSpec(memory_space=pltpu.VMEM)
    smem = pl.BlockSpec(memory_space=pltpu.SMEM)
    per_rows = (STREAMS, stream, rows)
    per_chip = (STREAMS, stream, chip_rows)
    per_feats = (STREAMS, stream, feats)
    residual, weights = pl.pallas_call(
        functools.partial(kernel, penalty),
        out_shape=[jax.ShapeDtypeStruct(per_chip, F32), jax.ShapeDtypeStruct(per_feats, F32)],
        in_specs=[smem] + [pl.BlockSpec(memory_space=pl.ANY)] * 4,
        out_specs=[vmem, vmem],
        scratch_shapes=[
            pltpu.VMEM((chip_rows, outs), F32),
            pltpu.VMEM((feats, outs), F32),
            pltpu.VMEM((blk // 4, feats), F32),
            pltpu.VMEM((chip_rows, feats), BF16),
            pltpu.VMEM((2, rows, feats), BF16),
            pltpu.VMEM((rows, feats), F32),
            pltpu.VMEM((rows, feats), F32),
            pltpu.VMEM(per_rows, F32),
            pltpu.VMEM(per_rows, BF16),
            pltpu.VMEM((outs, chip_rows), BF16),
            pltpu.VMEM(per_feats, F32),
            pltpu.VMEM((STREAMS, 2, 2, 7, quarter, blk), F32),
            pltpu.VMEM((STREAMS, 2, quarter, blk), F32),
            pltpu.VMEM((STREAMS, 2, 2, 3, quarter, blk), F32),
            pltpu.VMEM((STREAMS, 2, 2, 4, quarter, blk), F32),
            pltpu.VMEM((STREAMS, 2, stream, feats), F32),
            pltpu.VMEM(per_rows, F32),
            pltpu.VMEM((STREAMS, 2, stream, rows), F32),
            pltpu.VMEM(per_rows, F32),
            pltpu.VMEM((STREAMS, 2, stream, rows), F32),
            pltpu.VMEM(per_rows, F32),
            pltpu.VMEM(per_rows, F32),
            pltpu.VMEM((2, blk, blk), F32),
            pltpu.VMEM((2, blk, blk), BF16),
            pltpu.SemaphoreType.DMA((8,)),
            pltpu.SemaphoreType.DMA((STREAMS, 2)),
            pltpu.SemaphoreType.DMA((STREAMS, 2, N_SEM)),
            pltpu.SemaphoreType.DMA((8,)),
            pltpu.SemaphoreType.DMA((8,)),
            pltpu.SemaphoreType.DMA((PIECES + STREAMS,)),
            pltpu.SemaphoreType.DMA((PIECES + STREAMS,)),
            pltpu.SemaphoreType.DMA((STREAMS, CHUNKS)),
            pltpu.SemaphoreType.DMA((STREAMS, CHUNKS)),
        ],
        compiler_params=pltpu.CompilerParams(
            collective_id=0, has_side_effects=True, vmem_limit_bytes=56 * 1024 * 1024
        ),
        cost_estimate=pl.CostEstimate(
            flops=STEPS * 4 * rows * feats * outs, bytes_accessed=2 * chip_rows * feats, transcendentals=0
        ),
    )(order, samples, residual_in, weights_in, inverses[0])
    return weights.reshape(outs, feats).T, residual.reshape(outs, chip_rows).T


def solution(mesh):
    placed = (P("samp", "feat"), P("samp", None), P("feat", None), P("feat", "samp", None), P())
    return jax.shard_map(
        on_device,
        mesh=mesh,
        in_specs=placed,
        out_specs=(P("feat", None), P("samp", None)),
        check_vma=False,
    )
```
